32 devices in a mesh: dp: 4 (over z), section: 4 (over x, core), mp: 2 (over y).
Axes of the slice: x: 2, y: 2, z: 4, core: 2. Of those that a mesh axis runs over, the one named last changes fastest.
Arguments:
- act_in: bfloat16 [4, 1024, 4096], P('section', 'dp', 'mp'), may hold values from -6 to 6
- weights: bfloat16 [4, 4096, 4096], P('section', None, 'mp'), may hold values from -0.09375 to 0.09375
- act_saved: bfloat16 [4, 1024, 4096], P('section', 'dp', 'mp'), may hold values from -6 to 6
- cotangent: bfloat16 [4, 1024, 4096], P('section', 'dp', 'mp'), may hold values from -6 to 6
Outputs:
- received: bfloat16 [4, 1024, 4096], P('section', 'dp', 'mp')
- shadow: bfloat16 [4, 1024, 4096], P('section', 'dp', 'mp')
- grad_back: bfloat16 [4, 1024, 4096], P('section', 'dp', 'mp')
- weight_grad: bfloat16 [4, 4096, 4096], P('section', 'dp', 'mp')
The draws below stay inside these ranges and needn't reach their ends.
All inputs are finite; a program needn't handle non-finite values.
Results may differ from the reference program's by a relative error of at most 0.009.
Values may be sent and summed in bfloat16 or wider, within the bound.
No kernel may reach another device: no remote copies, remote signals or barrier semaphores. Data moves between devices by JAX's collectives and lax.ppermute only.
A program may use at most 192 MiB of HBM per device.

```python
import jax
import jax.numpy as jnp
from jax import lax

D = 4096
TOK_DEV = 256
SECTIONS = 4
TOKENS = 1024
N_DP = 4


def block_levels(own_key, shape, cuts, least, high):
    def one(axis_at, parts):
        heights = jax.random.uniform(jax.random.fold_in(jax.random.fold_in(own_key, 6), axis_at), (parts,), jnp.float32, least / len(cuts), high / len(cuts))
        return jnp.repeat(jnp.exp(heights), shape[axis_at] // parts).reshape((-1,) + (1,) * (len(shape) - axis_at - 1))

    gain = one(*cuts[0])
    for cut in cuts[1:]:
        gain = gain * one(*cut)
    return gain


def noise(own_key, shape, deviation, reach, shards=(), kind=jnp.bfloat16):
    values = deviation * jax.random.normal(own_key, shape, jnp.float32)
    if shards:
        values = values * block_levels(own_key, shape, shards, -0.22, 0.18)
    return jnp.clip(values, -reach, reach).astype(kind)


def setup_inputs(seed: int = 0) -> dict:
    streams_of = jax.random.split(jax.random.key(seed), 5)
    act_in = noise(streams_of[0], (SECTIONS, TOKENS, D), 1.0, 6.0, ((0, 4), (1, 4), (2, 2)))
    weights = noise(streams_of[1], (SECTIONS, D, D), D ** -0.5, 0.09375, ((0, 4), (2, 2)))
    act_saved = noise(streams_of[2], (SECTIONS, TOKENS, D), 1.0, 6.0, ((0, 4), (1, 4), (2, 2)))
    cotangent = noise(streams_of[3], (SECTIONS, TOKENS, D), 1.0, 6.0, ((0, 4), (1, 4), (2, 2)))
    return {"act_in": act_in, "weights": weights, "act_saved": act_saved, "cotangent": cotangent}


EPS = 1e-05

def normalize(rows):
    values = rows.astype(jnp.float32)
    average = lax.optimization_barrier(jnp.mean(values, axis=-1, keepdims=True))
    centred = values - average
    spread = lax.optimization_barrier(jnp.mean(centred * centred, axis=-1, keepdims=True))
    inverse = lax.rsqrt(spread + EPS)
    return (centred * inverse, inverse)

def forward_layer(rows, weight):
    scaled, inverse = normalize(rows)
    normed = scaled.astype(jnp.bfloat16)
    preact = jnp.dot(normed, weight, preferred_element_type=jnp.float32)
    return (rows.astype(jnp.float32) + jax.nn.gelu(preact)).astype(jnp.bfloat16)

def reference(act_in, weights, act_saved, cotangent):
    sections = act_in.shape[0]
    forward = [forward_layer(act_in[index], weights[index]) for index in range(sections)]
    received = jnp.stack([forward[(index - 1) % sections] for index in range(sections)])
    shadow = jnp.stack([forward_layer(forward[index], weights[(index + 1) % sections]) for index in range(sections)])
    input_grads = []
    weight_grads = []
    for index in range(sections):
        scaled, inverse = normalize(act_saved[index])
        normed = scaled.astype(jnp.bfloat16)
        preact = jnp.dot(normed, weights[index], preferred_element_type=jnp.float32)
        _, pullback = jax.vjp(jax.nn.gelu, preact)
        pre_grad = pullback(cotangent[index].astype(jnp.float32))[0].astype(jnp.bfloat16)
        total = jnp.zeros((D, D), jnp.float32)
        for replica in range(N_DP):
            rows = normed[replica * TOK_DEV:(replica + 1) * TOK_DEV]
            grads_part = pre_grad[replica * TOK_DEV:(replica + 1) * TOK_DEV]
            term = jnp.dot(rows.T, grads_part, preferred_element_type=jnp.float32)
            total = total + lax.optimization_barrier(term.astype(jnp.bfloat16)).astype(jnp.float32)
        weight_grads.append(total.astype(jnp.bfloat16))
        dnormed = jnp.dot(pre_grad, weights[index].T, preferred_element_type=jnp.float32)
        first = lax.optimization_barrier(jnp.mean(dnormed, axis=-1, keepdims=True))
        second = lax.optimization_barrier(jnp.mean(dnormed * scaled, axis=-1, keepdims=True))
        input_grad = cotangent[index].astype(jnp.float32) + inverse * (dnormed - first - scaled * second)
        input_grads.append(input_grad.astype(jnp.bfloat16))
    grad_back = jnp.stack([input_grads[(index + 1) % sections] for index in range(sections)])
    return (received, shadow, grad_back, jnp.stack(weight_grads))
```

```python
import jax
import jax.numpy as jnp
from jax import lax
from jax.sharding import PartitionSpec as P

EPS = 1e-05


def shift(value, axis, steps):
    count = lax.axis_size(axis)
    return lax.ppermute(value, axis, [(at, (at + steps) % count) for at in range(count)])


def swap(value, axis):
    return shift(value, axis, 1)


def line(value, axis, steps):
    count = lax.axis_size(axis)
    pairs = [(at, at + steps) for at in range(count) if 0 <= at + steps < count]
    return lax.ppermute(value, axis, pairs)


def shift_and_swap(value, steps):
    sections, halves = lax.axis_size("section"), lax.axis_size("mp")
    pairs = [
        (at * halves + half, ((at + steps) % sections) * halves + (half + 1) % halves)
        for at in range(sections)
        for half in range(halves)
    ]
    return lax.ppermute(value, ("section", "mp"), pairs)


def whole_rows(own, other):
    first = lax.axis_index("mp") == 0
    return jnp.concatenate([jnp.where(first, own, other), jnp.where(first, other, own)], axis=1)


def normalize(rows):
    values = rows.astype(jnp.float32)
    average = jnp.mean(values, axis=-1, keepdims=True)
    centred = values - average
    spread = jnp.mean(centred * centred, axis=-1, keepdims=True)
    inverse = lax.rsqrt(spread + EPS)
    return (centred * inverse, inverse)


def forward_layer(full_rows, own_rows, weight):
    normed = normalize(full_rows)[0].astype(jnp.bfloat16)
    preact = jnp.dot(normed, weight, preferred_element_type=jnp.float32)
    return (own_rows.astype(jnp.float32) + jax.nn.gelu(preact)).astype(jnp.bfloat16)


def body(act_in, weights, act_saved, cotangent):
    weight = weights[0]
    own_in, own_saved, own_cot = act_in[0], act_saved[0], cotangent[0]
    depth, columns = weight.shape
    replicas = lax.axis_size("dp")
    me_dp, me_mp = lax.axis_index("dp"), lax.axis_index("mp")
    own_at, other_at = me_mp * columns, (1 - me_mp) * columns
    block = depth // replicas

    other_saved = swap(own_saved, "mp")
    other_in = swap(own_in, "mp")

    scaled, inverse = normalize(whole_rows(own_saved, other_saved))
    normed = scaled.astype(jnp.bfloat16)
    normed_blocks = [lax.dynamic_slice_in_dim(normed, me_dp * block, block, 1)]
    for steps in range(1, replicas):
        target = (me_dp + steps) % replicas
        normed_blocks.append(
            shift(lax.dynamic_slice_in_dim(normed, target * block, block, 1), "dp", steps)
        )
    preact = jnp.dot(normed, weight, preferred_element_type=jnp.float32)
    _, pullback = jax.vjp(jax.nn.gelu, preact)
    pre_grad = pullback(own_cot.astype(jnp.float32))[0].astype(jnp.bfloat16)

    ups, downs = [pre_grad], [pre_grad]
    for _ in range(1, replicas):
        ups.append(line(ups[-1], "dp", 1))
        downs.append(line(downs[-1], "dp", -1))
    grads = [pre_grad] + [
        jnp.where(me_dp >= steps, ups[steps], downs[replicas - steps])
        for steps in range(1, replicas)
    ]

    part = lax.dot_general(
        pre_grad, weight, (((1,), (1,)), ((), ())), preferred_element_type=jnp.float32
    )
    sums = jnp.stack([jnp.sum(part, axis=-1), jnp.sum(part * scaled, axis=-1)])
    part_other = lax.dynamic_slice_in_dim(part, other_at, columns, 1).astype(jnp.bfloat16)
    part_own = lax.dynamic_slice_in_dim(part, own_at, columns, 1)
    sums = (sums + swap(sums, "mp")) / depth
    dnormed = part_own + swap(part_other, "mp").astype(jnp.float32)
    scaled_own = lax.dynamic_slice_in_dim(scaled, own_at, columns, 1)
    input_grad = own_cot.astype(jnp.float32) + inverse * (
        dnormed - sums[0][:, None] - scaled_own * sums[1][:, None]
    )
    grad_back = shift(input_grad.astype(jnp.bfloat16), "section", -1)

    forward = forward_layer(whole_rows(own_in, other_in), own_in, weight)
    received = shift(forward, "section", 1)
    received_other = shift_and_swap(forward, 1)
    shadow_there = forward_layer(whole_rows(received, received_other), received, weight)
    shadow = shift(shadow_there, "section", -1)

    weight_grad = lax.dot_general(
        jnp.concatenate(normed_blocks, axis=0),
        jnp.concatenate(grads, axis=0),
        (((0,), (0,)), ((), ())),
        preferred_element_type=jnp.float32,
    ).astype(jnp.bfloat16)
    return (received[None], shadow[None], grad_back[None], weight_grad[None])


def solution(mesh):
    return jax.shard_map(
        body,
        mesh=mesh,
        in_specs=(
            P("section", "dp", "mp"),
            P("section", None, "mp"),
            P("section", "dp", "mp"),
            P("section", "dp", "mp"),
        ),
        out_specs=(
            P("section", "dp", "mp"),
            P("section", "dp", "mp"),
            P("section", "dp", "mp"),
            P("section", "dp", "mp"),
        ),
        check_vma=False,
    )
```

```python
import functools

import jax
import jax.numpy as jnp
from jax import lax
from jax.experimental import pallas as pl
from jax.experimental.pallas import tpu as pltpu
from jax.sharding import PartitionSpec as P

EPS = 1e-05
BF16 = jnp.bfloat16
F32 = jnp.float32
VMEM_LIMIT = 12 * 2**20
CHUNKS = 2


def shift(value, axis, steps):
    count = lax.axis_size(axis)
    return lax.ppermute(value, axis, [(at, (at + steps) % count) for at in range(count)])


def swap(value, axis):
    return shift(value, axis, 1)


def line(value, axis, steps):
    count = lax.axis_size(axis)
    pairs = [(at, at + steps) for at in range(count) if 0 <= at + steps < count]
    return lax.ppermute(value, axis, pairs)


def shift_and_swap(value, steps):
    sections, halves = lax.axis_size("section"), lax.axis_size("mp")
    pairs = [
        (at * halves + half, ((at + steps) % sections) * halves + (half + 1) % halves)
        for at in range(sections)
        for half in range(halves)
    ]
    return lax.ppermute(value, ("section", "mp"), pairs)


VMEM = pl.BlockSpec(memory_space=pltpu.VMEM)
SMEM = pl.BlockSpec(memory_space=pltpu.SMEM)
ANY = pl.BlockSpec(memory_space=pl.ANY)


def call(kernel, name, place, values, outs, tokens=(), scratch=(), limit=VMEM_LIMIT):
    counted = len(values)

    def run(place_ref, *refs):
        kernel(place_ref, *refs[:counted], *refs[counted + len(tokens) :])

    return pl.pallas_call(
        run,
        in_specs=[SMEM] + [VMEM] * len(values) + [ANY] * len(tokens),
        out_specs=[VMEM] * len(outs),
        out_shape=outs,
        scratch_shapes=scratch,
        compiler_params=pltpu.CompilerParams(vmem_limit_bytes=limit),
        cost_estimate=pl.CostEstimate(flops=1000, bytes_accessed=1000, transcendentals=0),
        name=name,
    )(place, *values, *tokens)


def array(rows, columns, dtype=BF16):
    return jax.ShapeDtypeStruct((rows, columns), dtype)


def gelu(v):
    scale = 0.7978845608028654
    return 0.5 * v * (1.0 + jnp.tanh(scale * (v + 0.044715 * (v * v * v))))


def gelu_slope(v):
    scale = 0.7978845608028654
    square = v * v
    t = jnp.tanh(scale * (v + 0.044715 * (square * v)))
    return 0.5 * (1.0 + t) + 0.5 * v * (1.0 - t * t) * (scale * (1.0 + 3 * 0.044715 * square))


def normalize_into(own_ref, other_ref, normed_ref, half, own_start=0, step=128):
    rows, columns = other_ref.shape
    own_at = pl.multiple_of(half * columns, columns)
    other_at = pl.multiple_of((1 - half) * columns, columns)
    inverses = []
    for start in range(0, rows, step):
        at = slice(start, start + step)
        own = own_ref[own_start + start : own_start + start + step, :].astype(F32)
        other = other_ref[at, :].astype(F32)
        total = jnp.sum(own, axis=-1, keepdims=True) + jnp.sum(other, axis=-1, keepdims=True)
        average = total / (2 * columns)
        own, other = own - average, other - average
        total = jnp.sum(own * own, axis=-1, keepdims=True)
        total = total + jnp.sum(other * other, axis=-1, keepdims=True)
        inverse = lax.rsqrt(total / (2 * columns) + EPS)
        normed_ref[at, pl.ds(own_at, columns)] = (own * inverse).astype(BF16)
        normed_ref[at, pl.ds(other_at, columns)] = (other * inverse).astype(BF16)
        inverses.append(inverse)
    return inverses


def norm_kernel(replicas, chunk, place_ref, own_ref, other_ref, normed_ref, inverse_ref, *block_refs):
    rows = other_ref.shape[0]
    (inverse,) = normalize_into(own_ref, other_ref, normed_ref, place_ref[1], chunk * rows, rows)
    inverse_ref[...] = jnp.broadcast_to(inverse, inverse_ref.shape)
    block = block_refs[0].shape[1]
    for steps in range(replicas):
        target = lax.rem(place_ref[0] + steps, replicas)
        block_refs[steps][...] = normed_ref[:, pl.ds(pl.multiple_of(target * block, block), block)]


def norm_blocks(place, own, other, replicas, chunk, tokens=()):
    rows, columns = other.shape
    outs = [array(rows, 2 * columns), array(rows, 128, F32)]
    outs += [array(rows, 2 * columns // replicas)] * replicas
    kernel = functools.partial(norm_kernel, replicas, chunk)
    return call(kernel, "norm_blocks", place, [own, other], outs, tokens)


def later_kernel(place_ref, value_ref, *refs):
    refs[-1][...] = value_ref[...]


def later(place, value, tokens):
    return call(later_kernel, "later", place, [value], [array(*value.shape)], tokens)[0]


def load_kernel(place_ref, weight_ref, held_ref, sem):
    copy = pltpu.make_async_copy(weight_ref, held_ref, sem)
    copy.start()
    copy.wait()


def load(place, weight):
    held = pl.pallas_call(
        load_kernel,
        in_specs=[SMEM, ANY],
        out_specs=VMEM,
        out_shape=pltpu.VMEM(weight.shape, weight.dtype),
        scratch_shapes=[pltpu.SemaphoreType.DMA],
        compiler_params=pltpu.CompilerParams(vmem_limit_bytes=VMEM_LIMIT),
        name="load_weights",
    )(place, weight)
    return pltpu.with_memory_space_constraint(held, pltpu.VMEM)


def pre_grad_kernel(chunk, place_ref, normed_ref, weight_ref, cot_ref, grad_ref, tile=256):
    rows = grad_ref.shape[0]
    for start in range(0, grad_ref.shape[1], tile):
        at = slice(start, start + tile)
        preact = jnp.dot(normed_ref[...], weight_ref[:, at], preferred_element_type=F32)
        cot = cot_ref[chunk * rows : (chunk + 1) * rows, at].astype(F32)
        grad_ref[:, at] = (cot * gelu_slope(preact)).astype(BF16)


def pre_grads(place, normed, weight, cot, chunk, tokens=()):
    outs = [array(normed.shape[0], weight.shape[1])]
    kernel = functools.partial(pre_grad_kernel, chunk)
    return call(kernel, "pre_grads", place, [normed, weight, cot], outs, tokens)[0]


def forward_kernel(place_ref, own_ref, other_ref, weight_ref, out_ref, normed_ref, tile=256):
    normalize_into(own_ref, other_ref, normed_ref, place_ref[1])
    for start in range(0, out_ref.shape[1], tile):
        at = slice(start, start + tile)
        preact = jnp.dot(normed_ref[...], weight_ref[:, at], preferred_element_type=F32)
        out_ref[:, at] = (own_ref[:, at].astype(F32) + gelu(preact)).astype(BF16)


def forward_layer(place, own, other, weight, tokens=()):
    scratch = [pltpu.VMEM((own.shape[0], weight.shape[0]), BF16)]
    return call(
        forward_kernel, "forward_layer", place, [own, other, weight], [array(*own.shape)], tokens, scratch
    )[0]


def dnormed_kernel(chunks, place_ref, *refs, tile=512):
    grad_refs, normed_refs = refs[:chunks], refs[chunks : 2 * chunks]
    weight_ref, send_ref, keep_ref, sums_ref = refs[2 * chunks :]
    rows = grad_refs[0].shape[0]
    depth, columns = weight_ref.shape
    lane = lax.broadcasted_iota(jnp.int32, (rows, sums_ref.shape[1]), 1)
    for chunk in range(chunks):
        at = slice(chunk * rows, (chunk + 1) * rows)
        first = second = jnp.zeros((rows, 1), F32)
        for mine in (False, True):
            half = place_ref[1] if mine else 1 - place_ref[1]
            for start in range(0, columns, tile):
                features = pl.ds(pl.multiple_of(half * columns + start, tile), tile)
                part = lax.dot_general(
                    grad_refs[chunk][...],
                    weight_ref[features, :],
                    (((1,), (1,)), ((), ())),
                    preferred_element_type=F32,
                )
                first += jnp.sum(part, axis=-1, keepdims=True)
                scaled = normed_refs[chunk][:, features].astype(F32)
                second += jnp.sum(part * scaled, axis=-1, keepdims=True)
                if mine:
                    keep_ref[at, start : start + tile] = part
                else:
                    send_ref[at, start : start + tile] = part.astype(BF16)
        sums_ref[at, :] = jnp.where(lane < 64, first, second)


def dnormed_parts(place, grads, normeds, weight, tokens=()):
    chunks = len(grads)
    rows, columns = chunks * grads[0].shape[0], weight.shape[1]
    outs = [array(rows, columns), array(rows, columns, F32), array(rows, 128, F32)]
    kernel = functools.partial(dnormed_kernel, chunks)
    return call(kernel, "dnormed_parts", place, [*grads, *normeds, weight], outs, tokens)


def input_grad_kernel(chunks, place_ref, cot_ref, keep_ref, arrived_ref, sums_ref, other_sums_ref, *refs):
    inverse_refs, normed_refs, out_ref = refs[:chunks], refs[chunks : 2 * chunks], refs[-1]
    rows = inverse_refs[0].shape[0]
    columns = cot_ref.shape[1]
    depth = 2 * columns
    mine = pl.ds(pl.multiple_of(place_ref[1] * columns, columns), columns)
    for chunk in range(chunks):
        at = slice(chunk * rows, (chunk + 1) * rows)
        sums = (sums_ref[at, :] + other_sums_ref[at, :]) / depth
        first, second = sums[:, 0:1], sums[:, 64:65]
        dnormed = keep_ref[at, :] + arrived_ref[at, :].astype(F32)
        scaled = normed_refs[chunk][:, mine].astype(F32)
        out_ref[at, :] = (
            cot_ref[at, :].astype(F32)
            + inverse_refs[chunk][:, 0:1] * (dnormed - first - scaled * second)
        ).astype(BF16)


def input_grads(place, cot, keep, arrived, sums, other_sums, inverses, normeds, tokens=()):
    values = [cot, keep, arrived, sums, other_sums, *inverses, *normeds]
    kernel = functools.partial(input_grad_kernel, len(inverses))
    return call(kernel, "input_grads", place, values, [array(*cot.shape)], tokens)[0]


def weight_grad_kernel(replicas, chunks, place_ref, *refs, tile=256):
    count = replicas * chunks
    block_refs, up_refs, down_refs = refs[:count], refs[count : 2 * count], refs[2 * count : -3]
    out_ref, blocks, grads = refs[-3:]
    rows = block_refs[0].shape[0]
    for index in range(count):
        at = slice(index * rows, (index + 1) * rows)
        blocks[at, :] = block_refs[index][...]
        steps = index // chunks
        if steps == 0:
            grads[at, :] = up_refs[index][...]
        else:
            grads[at, :] = jnp.where(
                place_ref[0] >= steps, up_refs[index][...], down_refs[index - chunks][...]
            )
    for start in range(0, out_ref.shape[0], tile):
        at = slice(start, start + tile)
        out_ref[at, :] = lax.dot_general(
            blocks[:, at], grads[...], (((0,), (0,)), ((), ())), preferred_element_type=F32
        ).astype(BF16)


def weight_grads(place, blocks, ups, downs, replicas, chunks, tokens=()):
    rows, depth = blocks[0].shape
    columns = ups[0].shape[1]
    count = replicas * chunks
    scratch = [pltpu.VMEM((count * rows, depth), BF16), pltpu.VMEM((count * rows, columns), BF16)]
    kernel = functools.partial(weight_grad_kernel, replicas, chunks)
    values = [*blocks, *ups, *downs[chunks:]]
    return call(kernel, "weight_grads", place, values, [array(depth, columns)], tokens, scratch, 28 * 2**20)[0]


def body(act_in, weights, act_saved, cotangent):
    weight = weights[0]
    own_in, own_saved, own_cot = act_in[0], act_saved[0], cotangent[0]
    rows = own_saved.shape[0] // CHUNKS
    replicas = lax.axis_size("dp")
    place = jnp.stack([lax.axis_index("dp"), lax.axis_index("mp")]).astype(jnp.int32)

    other_saved = [swap(own_saved[chunk * rows : (chunk + 1) * rows], "mp") for chunk in range(CHUNKS)]
    weight = load(place, weight)

    normeds, inverses, blocks, ups, downs = [], [], [], [], []
    tokens = [weight]
    for chunk in range(CHUNKS):
        normed, inverse, own_block, *away = norm_blocks(
            place, own_saved, other_saved[chunk], replicas, chunk, tokens
        )
        normeds.append(normed)
        inverses.append(inverse)
        blocks.append([own_block] + [shift(value, "dp", steps + 1) for steps, value in enumerate(away)])
        if chunk == 0:
            other_in = swap(later(place, own_in, [inverse]), "mp")
        pre_grad = pre_grads(place, normed, weight, own_cot, chunk)
        up, down = [pre_grad], [pre_grad]
        for _ in range(1, replicas):
            up.append(line(up[-1], "dp", 1))
            down.append(line(down[-1], "dp", -1))
        ups.append(up)
        downs.append(down)
        tokens = blocks[0][1:2]

    send, keep, sums = dnormed_parts(place, [up[0] for up in ups], normeds, weight, blocks[0][2:])
    arrived, other_sums = swap(send, "mp"), swap(sums, "mp")

    forward = forward_layer(place, own_in, other_in, weight, [ups[0][1], downs[0][1]])
    received = shift(forward, "section", 1)
    received_other = shift_and_swap(forward, 1)

    input_grad = input_grads(
        place, own_cot, keep, arrived, sums, other_sums, inverses, normeds, blocks[1][1:]
    )
    grad_back = shift(input_grad, "section", -1)

    shadow_there = forward_layer(
        place,
        received,
        received_other,
        weight,
        [ups[1][1], downs[1][1], ups[0][2], downs[0][2], input_grad],
    )
    shadow = shift(shadow_there, "section", -1)

    order = [(steps, chunk) for steps in range(replicas) for chunk in range(CHUNKS)]
    weight_grad = weight_grads(
        place,
        [blocks[chunk][steps] for steps, chunk in order],
        [ups[chunk][steps] for steps, chunk in order],
        [downs[chunk][(replicas - steps) % replicas] for steps, chunk in order],
        replicas,
        CHUNKS,
        [shadow_there],
    )
    return (received[None], shadow[None], grad_back[None], weight_grad[None])


def solution(mesh):
    return jax.shard_map(
        body,
        mesh=mesh,
        in_specs=(
            P("section", "dp", "mp"),
            P("section", None, "mp"),
            P("section", "dp", "mp"),
            P("section", "dp", "mp"),
        ),
        out_specs=(
            P("section", "dp", "mp"),
            P("section", "dp", "mp"),
            P("section", "dp", "mp"),
            P("section", "dp", "mp"),
        ),
        check_vma=False,
    )
```

```python
import functools

import jax
import jax.numpy as jnp
from jax import lax
from jax.experimental import pallas as pl
from jax.experimental.pallas import tpu as pltpu
from jax.sharding import PartitionSpec as P

EPS = 1e-05
BF16 = jnp.bfloat16
F32 = jnp.float32
VMEM_LIMIT = 12 * 2**20


def shift(value, axis, steps):
    count = lax.axis_size(axis)
    return lax.ppermute(value, axis, [(at, (at + steps) % count) for at in range(count)])


def swap(value, axis):
    return shift(value, axis, 1)


def along(value, axis, steps, skipped=0):
    count = lax.axis_size(axis)
    held = range(skipped, count) if steps > 0 else range(count - skipped)
    pairs = [(at, at + steps) for at in held if 0 <= at + steps < count]
    return lax.ppermute(value, axis, pairs)


def across(value, axis, steps):
    count = lax.axis_size(axis)
    pairs = [(at, at + steps) for at in range(count - steps)]
    return lax.ppermute(value, axis, pairs + [(target, source) for source, target in pairs])


def shift_and_swap(value, steps):
    sections, halves = lax.axis_size("section"), lax.axis_size("mp")
    pairs = [
        (at * halves + half, ((at + steps) % sections) * halves + (half + 1) % halves)
        for at in range(sections)
        for half in range(halves)
    ]
    return lax.ppermute(value, ("section", "mp"), pairs)


VMEM = pl.BlockSpec(memory_space=pltpu.VMEM)
SMEM = pl.BlockSpec(memory_space=pltpu.SMEM)
ANY = pl.BlockSpec(memory_space=pl.ANY)


def call(kernel, name, place, values, outs, tokens=(), scratch=(), limit=VMEM_LIMIT, flops=1000):
    counted = len(values)

    def run(place_ref, *refs):
        kernel(place_ref, *refs[:counted], *refs[counted + len(tokens) :])

    return pl.pallas_call(
        run,
        in_specs=[SMEM] + [VMEM] * len(values) + [ANY] * len(tokens),
        out_specs=[VMEM] * len(outs),
        out_shape=outs,
        scratch_shapes=scratch,
        compiler_params=pltpu.CompilerParams(vmem_limit_bytes=limit),
        cost_estimate=pl.CostEstimate(flops=flops, bytes_accessed=1000, transcendentals=0),
        name=name,
    )(place, *values, *tokens)


def array(*shape):
    dtype = shape[-1] if shape[-1] is F32 else BF16
    return jax.ShapeDtypeStruct(tuple(size for size in shape if size is not F32), dtype)


def gelu(v):
    scale = 0.7978845608028654
    return 0.5 * v * (1.0 + jnp.tanh(scale * (v + 0.044715 * (v * v * v))))


def gelu_slope(v):
    scale = 0.7978845608028654
    square = v * v
    t = jnp.tanh(scale * (v + 0.044715 * (square * v)))
    return 0.5 * (1.0 + t) + 0.5 * v * (1.0 - t * t) * (scale * (1.0 + 3 * 0.044715 * square))


def normalize_into(own_ref, other_ref, normed_ref, half, own_start=0, step=128):
    rows, columns = other_ref.shape
    own_at = pl.multiple_of(half * columns, columns)
    other_at = pl.multiple_of((1 - half) * columns, columns)
    inverses = []
    for start in range(0, rows, step):
        at = slice(start, start + step)
        own = own_ref[own_start + start : own_start + start + step, :].astype(F32)
        other = other_ref[at, :].astype(F32)
        total = jnp.sum(own, axis=-1, keepdims=True) + jnp.sum(other, axis=-1, keepdims=True)
        average = total / (2 * columns)
        own, other = own - average, other - average
        total = jnp.sum(own * own, axis=-1, keepdims=True)
        total = total + jnp.sum(other * other, axis=-1, keepdims=True)
        inverse = lax.rsqrt(total / (2 * columns) + EPS)
        normed_ref[at, pl.ds(own_at, columns)] = (own * inverse).astype(BF16)
        normed_ref[at, pl.ds(other_at, columns)] = (other * inverse).astype(BF16)
        inverses.append(inverse)
    return inverses


def split_blocks(place_ref, normed_ref, rows, block_refs, replicas, first=0):
    block = block_refs[0].shape[1]
    for steps in range(first, len(block_refs)):
        target = lax.rem(place_ref[0] + steps, replicas)
        block_refs[steps][...] = normed_ref[rows, pl.ds(pl.multiple_of(target * block, block), block)]


def norm_kernel(place_ref, own_ref, other_ref, normed_ref, inverse_ref, scaled_ref, *block_refs):
    rows, columns = own_ref.shape
    half = place_ref[1]
    for index, inverse in enumerate(normalize_into(own_ref, other_ref, normed_ref, half)):
        at = slice(index * 128, (index + 1) * 128)
        inverse_ref[at, :] = jnp.broadcast_to(inverse, (128, inverse_ref.shape[1]))
    scaled_ref[...] = normed_ref[:, pl.ds(pl.multiple_of(half * columns, columns), columns)]
    part = rows // 2
    split_blocks(place_ref, normed_ref, slice(None), block_refs[:1], len(block_refs))
    mine = pl.ds(pl.multiple_of(half * part, part), part)
    split_blocks(place_ref, normed_ref, mine, block_refs, len(block_refs), 1)


def norm_rows(place, own, other, replicas, tokens=()):
    rows, columns = own.shape
    block = 2 * columns // replicas
    outs = [array(rows, 2 * columns), array(rows, 128, F32), array(rows, columns), array(rows, block)]
    outs += [array(rows // 2, block)] * (replicas - 1)
    return call(norm_kernel, "norm_rows", place, [own, other], outs, tokens)


def backward_kernel(
    place_ref, normed_ref, weight_ref, cot_ref, grad_ref, send_ref, keep_ref, sums_ref, tile=512
):
    rows, columns = cot_ref.shape
    half = place_ref[1]
    for start in range(0, columns, tile):
        at = slice(start, start + tile)
        preact = jnp.dot(normed_ref[...], weight_ref[:, at], preferred_element_type=F32)
        grad_ref[:, at] = (cot_ref[:, at].astype(F32) * gelu_slope(preact)).astype(BF16)
    first = jnp.zeros((rows, 1), F32)
    second = jnp.zeros((rows, 1), F32)
    for is_mine in (False, True):
        at_half = half if is_mine else 1 - half
        for start in range(0, columns, tile):
            features = pl.ds(pl.multiple_of(at_half * columns + start, tile), tile)
            part = lax.dot_general(
                grad_ref[...], weight_ref[features, :], (((1,), (1,)), ((), ())), preferred_element_type=F32
            )
            first += jnp.sum(part, axis=-1, keepdims=True)
            second += jnp.sum(part * normed_ref[:, features].astype(F32), axis=-1, keepdims=True)
            if is_mine:
                keep_ref[:, start : start + tile] = part
            else:
                send_ref[:, start : start + tile] = part.astype(BF16)
    lane = lax.broadcasted_iota(jnp.int32, (rows, 128), 1)
    left = jnp.where(lane < 64, first, second)
    sums_ref[...] = left
    terms = jnp.zeros((rows, 128), F32)
    for index in range(3):
        term = left.astype(BF16).astype(F32)
        left = left - term
        terms = jnp.where(lane % 64 // 16 == index, term, terms)
    send_ref[:, columns : columns + 128] = terms.astype(BF16)


def backward_rows(place, normed, weight, cot, tokens=()):
    rows, columns = cot.shape
    outs = [array(rows, columns), array(rows, columns + 128), array(rows, columns, F32), array(rows, 128, F32)]
    return call(backward_kernel, "backward_rows", place, [normed, weight, cot], outs, tokens)


def stack_kernel(place_ref, *refs):
    rows = refs[0].shape[0]
    for index, ref in enumerate(refs[:-1]):
        refs[-1][index * rows : (index + 1) * rows, :] = ref[...]


def stack(place, values, tokens=()):
    rows, columns = values[0].shape
    return call(stack_kernel, "stack_blocks", place, values, [array(len(values) * rows, columns)], tokens)[0]


def load_kernel(place_ref, weight_ref, held_ref, sem):
    copy = pltpu.make_async_copy(weight_ref, held_ref, sem)
    copy.start()
    copy.wait()


def load(place, weight):
    held = pl.pallas_call(
        load_kernel,
        in_specs=[SMEM, ANY],
        out_specs=VMEM,
        out_shape=pltpu.VMEM(weight.shape, weight.dtype),
        scratch_shapes=[pltpu.SemaphoreType.DMA],
        compiler_params=pltpu.CompilerParams(vmem_limit_bytes=VMEM_LIMIT),
        name="load_weights",
    )(place, weight)
    return pltpu.with_memory_space_constraint(held, pltpu.VMEM)


def forward_kernel(place_ref, own_ref, other_ref, weight_ref, out_ref, normed_ref, tile=256):
    normalize_into(own_ref, other_ref, normed_ref, place_ref[1])
    for start in range(0, out_ref.shape[1], tile):
        at = slice(start, start + tile)
        preact = jnp.dot(normed_ref[...], weight_ref[:, at], preferred_element_type=F32)
        out_ref[:, at] = (own_ref[:, at].astype(F32) + gelu(preact)).astype(BF16)


def forward_layer(place, own, other, weight, tokens=()):
    scratch = [pltpu.VMEM((own.shape[0], weight.shape[0]), BF16)]
    return call(
        forward_kernel, "forward_layer", place, [own, other, weight], [array(*own.shape)], tokens, scratch
    )[0]


def input_grad_kernel(
    place_ref, cot_ref, keep_ref, arrived_ref, sums_ref, inverse_ref, scaled_ref, out_ref
):
    columns = cot_ref.shape[1]
    depth = 2 * columns
    terms = arrived_ref[:, columns : columns + 128].astype(F32)
    first = sums_ref[:, 0:1] + ((terms[:, 0:1] + terms[:, 16:17]) + terms[:, 32:33])
    second = sums_ref[:, 64:65] + ((terms[:, 64:65] + terms[:, 80:81]) + terms[:, 96:97])
    dnormed = keep_ref[...] + arrived_ref[:, :columns].astype(F32)
    scaled = scaled_ref[...].astype(F32)
    out_ref[...] = (
        cot_ref[...].astype(F32)
        + inverse_ref[:, 0:1] * (dnormed - first / depth - scaled * (second / depth))
    ).astype(BF16)


def input_grads(place, cot, keep, arrived, sums, inverse, scaled, tokens=()):
    values = [cot, keep, arrived, sums, inverse, scaled]
    return call(input_grad_kernel, "input_grads", place, values, [array(*cot.shape)], tokens)[0]


def gather_kernel(replicas, place_ref, own_ref, *refs):
    near_refs, (far_ref, out_ref, blocks) = refs[: replicas - 1], refs[replicas - 1 :]
    rows = own_ref.shape[0]
    part = rows // 2
    half = place_ref[1]
    blocks[:rows, :] = own_ref[...]
    for steps in range(1, replicas):
        near = pl.ds(pl.multiple_of(rows * steps + half * part, part), part)
        far = pl.ds(pl.multiple_of(rows * steps + (1 - half) * part, part), part)
        blocks[near, :] = near_refs[steps - 1][...]
        blocks[far, :] = far_ref[(steps - 1) * part : steps * part, :]
    out_ref[...] = blocks[...].T


def gather_blocks(place, own, near, far):
    replicas = len(near) + 1
    rows, block = own.shape
    kernel = functools.partial(gather_kernel, replicas)
    scratch = [pltpu.VMEM((replicas * rows, block), BF16)]
    outs = [array(block, replicas * rows)]
    return call(
        kernel, "gather_blocks", place, [own, *near, far], outs, (), scratch
    )[0]


def gather_grad_kernel(place_ref, own_ref, *refs):
    *refs, out_ref = refs
    others = len(refs) // 2
    rows = own_ref.shape[0]
    out_ref[:rows, :] = own_ref[...]
    for steps in range(1, others + 1):
        out_ref[rows * steps : rows * (steps + 1), :] = jnp.where(
            place_ref[0] >= steps, refs[steps - 1][...], refs[others + steps - 1][...]
        )


def gather_grads(place, own, ups, downs):
    values = [own, *ups, *downs]
    outs = [array((len(ups) + 1) * own.shape[0], own.shape[1])]
    return call(
        gather_grad_kernel, "gather_grads", place, values, outs, limit=16 * 2**20, flops=3 * 10**10
    )[0]


def weight_grad_kernel(passed, place_ref, *refs, width=512):
    blocks_ref, grads_ref, *refs = refs
    pass_refs, out_ref, pass_outs = refs[:passed], refs[passed], refs[passed + 1 : 2 * passed + 1]
    held, sems, pass_sems = refs[-3:]
    passing = [
        pltpu.make_async_copy(pass_refs[at], pass_outs[at], pass_sems.at[at]) for at in range(passed)
    ]
    for copy in passing:
        copy.start()
    stores = []
    for index, start in enumerate(range(0, grads_ref.shape[1], width)):
        at = slice(start, start + width)
        held[:, at] = jnp.dot(
            blocks_ref[...], grads_ref[:, at], preferred_element_type=F32
        ).astype(BF16)
        stores.append(pltpu.make_async_copy(held.at[:, at], out_ref.at[:, at], sems.at[index]))
        stores[-1].start()
    for copy in stores + passing:
        copy.wait()


def weight_grads(place, blocks, grads, passes, width=512, limit=20 * 2**20):
    block, columns = blocks.shape[0], grads.shape[1]
    outs = [array(block, columns)] + [array(*value.shape) for value in passes]
    return pl.pallas_call(
        functools.partial(weight_grad_kernel, len(passes), width=width),
        in_specs=[SMEM] + [VMEM] * (2 + len(passes)),
        out_specs=[ANY] * len(outs),
        out_shape=outs,
        scratch_shapes=[
            pltpu.VMEM((block, columns), BF16),
            pltpu.SemaphoreType.DMA((columns // width,)),
            pltpu.SemaphoreType.DMA((len(passes),)),
        ],
        compiler_params=pltpu.CompilerParams(vmem_limit_bytes=limit),
        cost_estimate=pl.CostEstimate(flops=1000, bytes_accessed=1000, transcendentals=0),
        name="weight_grads",
    )(place, blocks, grads, *passes)


def after(value, *others):
    return lax.optimization_barrier((value, *others))[0]


def body(act_in, weights, act_saved, cotangent):
    weight = weights[0]
    own_in, own_saved, own_cot = act_in[0], act_saved[0], cotangent[0]
    replicas = lax.axis_size("dp")
    place = jnp.stack([lax.axis_index("dp"), lax.axis_index("mp")]).astype(jnp.int32)

    other_saved = swap(own_saved, "mp")
    weight = load(place, weight)
    other_in = swap(after(own_in, weight), "mp")

    normed, inverse, scaled, own_block, *blocks = norm_rows(
        place, own_saved, other_saved, replicas, [weight]
    )
    near = [shift(block, "dp", steps + 1) for steps, block in enumerate(blocks)]
    grad, send, keep, sums = backward_rows(place, normed, weight, own_cot)

    grad = after(grad, *near)
    arrived = swap(after(send, other_in, *near), "mp")
    ups, downs = [grad], [grad]
    for steps in range(1, replicas):
        if steps <= replicas // 2:
            ups.append(along(ups[-1], "dp", 1, steps - 1))
            downs.append(along(downs[-1], "dp", -1, steps - 1))
        else:
            ups.append(across(after(grad, ups[1], downs[1]), "dp", steps))
            downs.append(ups[-1])

    forward = forward_layer(place, own_in, other_in, weight)
    received = shift(after(forward, *near), "section", 1)
    received_other = shift_and_swap(after(forward, arrived), 1)

    far = swap(after(stack(place, near), received_other), "mp")
    shadow_there = forward_layer(place, received, received_other, weight)
    shadow = shift(shadow_there, "section", -1)

    input_grad = input_grads(place, own_cot, keep, arrived, sums, inverse, scaled)
    grad_back = shift(after(input_grad, received_other), "section", -1)

    weight_grad, received, shadow, grad_back = weight_grads(
        place,
        gather_blocks(place, own_block, near, far),
        gather_grads(place, grad, ups[1:], downs[:0:-1]),
        [received, shadow, grad_back],
    )
    return (received[None], shadow[None], grad_back[None], weight_grad[None])


def solution(mesh):
    return jax.shard_map(
        body,
        mesh=mesh,
        in_specs=(
            P("section", "dp", "mp"),
            P("section", None, "mp"),
            P("section", "dp", "mp"),
            P("section", "dp", "mp"),
        ),
        out_specs=(
            P("section", "dp", "mp"),
            P("section", "dp", "mp"),
            P("section", "dp", "mp"),
            P("section", "dp", "mp"),
        ),
        check_vma=False,
    )
```

```python
import functools

import jax
import jax.numpy as jnp
from jax import lax
from jax.experimental import pallas as pl
from jax.experimental.pallas import tpu as pltpu
from jax.sharding import PartitionSpec as P

EPS = 1e-05
BF16 = jnp.bfloat16
F32 = jnp.float32
VMEM_LIMIT = 12 * 2**20


def shift(value, axis, steps):
    count = lax.axis_size(axis)
    return lax.ppermute(value, axis, [(at, (at + steps) % count) for at in range(count)])


def swap(value, axis):
    return shift(value, axis, 1)


def along(value, axis, steps, skipped=0):
    count = lax.axis_size(axis)
    held = range(skipped, count) if steps > 0 else range(count - skipped)
    pairs = [(at, at + steps) for at in held if 0 <= at + steps < count]
    return lax.ppermute(value, axis, pairs)


def across(value, axis, steps):
    count = lax.axis_size(axis)
    pairs = [(at, at + steps) for at in range(count - steps)]
    return lax.ppermute(value, axis, pairs + [(target, source) for source, target in pairs])


def shift_and_swap(value, steps):
    sections, halves = lax.axis_size("section"), lax.axis_size("mp")
    pairs = [
        (at * halves + half, ((at + steps) % sections) * halves + (half + 1) % halves)
        for at in range(sections)
        for half in range(halves)
    ]
    return lax.ppermute(value, ("section", "mp"), pairs)


VMEM = pl.BlockSpec(memory_space=pltpu.VMEM)
SMEM = pl.BlockSpec(memory_space=pltpu.SMEM)
ANY = pl.BlockSpec(memory_space=pl.ANY)


def call(kernel, name, place, values, outs, tokens=(), scratch=(), limit=VMEM_LIMIT, flops=1000):
    counted = len(values)

    def run(place_ref, *refs):
        kernel(place_ref, *refs[:counted], *refs[counted + len(tokens) :])

    return pl.pallas_call(
        run,
        in_specs=[SMEM] + [VMEM] * len(values) + [ANY] * len(tokens),
        out_specs=[VMEM] * len(outs),
        out_shape=outs,
        scratch_shapes=scratch,
        compiler_params=pltpu.CompilerParams(vmem_limit_bytes=limit),
        cost_estimate=pl.CostEstimate(flops=flops, bytes_accessed=1000, transcendentals=0),
        name=name,
    )(place, *values, *tokens)


def array(*shape):
    dtype = shape[-1] if shape[-1] is F32 else BF16
    return jax.ShapeDtypeStruct(tuple(size for size in shape if size is not F32), dtype)


def gelu(v):
    scale = 0.7978845608028654
    return 0.5 * v * (1.0 + jnp.tanh(scale * (v + 0.044715 * (v * v * v))))


def gelu_slope(v):
    scale = 0.7978845608028654
    square = v * v
    t = jnp.tanh(scale * (v + 0.044715 * (square * v)))
    return 0.5 * (1.0 + t) + 0.5 * v * (1.0 - t * t) * (scale * (1.0 + 3 * 0.044715 * square))


def normalize_into(own_ref, other_ref, normed_ref, half, own_start=0, step=128):
    rows, columns = other_ref.shape
    own_at = pl.multiple_of(half * columns, columns)
    other_at = pl.multiple_of((1 - half) * columns, columns)
    inverses = []
    for start in range(0, rows, step):
        at = slice(start, start + step)
        own = own_ref[own_start + start : own_start + start + step, :].astype(F32)
        other = other_ref[at, :].astype(F32)
        total = jnp.sum(own, axis=-1, keepdims=True) + jnp.sum(other, axis=-1, keepdims=True)
        average = total / (2 * columns)
        own, other = own - average, other - average
        total = jnp.sum(own * own, axis=-1, keepdims=True)
        total = total + jnp.sum(other * other, axis=-1, keepdims=True)
        inverse = lax.rsqrt(total / (2 * columns) + EPS)
        normed_ref[at, pl.ds(own_at, columns)] = (own * inverse).astype(BF16)
        normed_ref[at, pl.ds(other_at, columns)] = (other * inverse).astype(BF16)
        inverses.append(inverse)
    return inverses


def split_blocks(place_ref, normed_ref, rows, block_refs, replicas, first=0):
    block = block_refs[0].shape[1]
    for steps in range(first, len(block_refs)):
        target = lax.rem(place_ref[0] + steps, replicas)
        block_refs[steps][...] = normed_ref[rows, pl.ds(pl.multiple_of(target * block, block), block)]


def norm_kernel(place_ref, own_ref, other_ref, normed_ref, inverse_ref, scaled_ref, *block_refs):
    rows, columns = own_ref.shape
    half = place_ref[1]
    for index, inverse in enumerate(normalize_into(own_ref, other_ref, normed_ref, half)):
        at = slice(index * 128, (index + 1) * 128)
        inverse_ref[at, :] = jnp.broadcast_to(inverse, (128, inverse_ref.shape[1]))
    scaled_ref[...] = normed_ref[:, pl.ds(pl.multiple_of(half * columns, columns), columns)]
    part = rows // 2
    split_blocks(place_ref, normed_ref, slice(None), block_refs[:1], len(block_refs))
    mine = pl.ds(pl.multiple_of(half * part, part), part)
    split_blocks(place_ref, normed_ref, mine, block_refs, len(block_refs), 1)


def norm_rows(place, own, other, replicas, tokens=()):
    rows, columns = own.shape
    block = 2 * columns // replicas
    outs = [array(rows, 2 * columns), array(rows, 128, F32), array(rows, columns), array(rows, block)]
    outs += [array(rows // 2, block)] * (replicas - 1)
    return call(norm_kernel, "norm_rows", place, [own, other], outs, tokens)


def backward_kernel(
    place_ref, normed_ref, weight_ref, cot_ref, grad_ref, send_ref, keep_ref, sums_ref, tile=512
):
    rows, columns = cot_ref.shape
    half = place_ref[1]
    for start in range(0, columns, tile):
        at = slice(start, start + tile)
        preact = jnp.dot(normed_ref[...], weight_ref[:, at], preferred_element_type=F32)
        grad_ref[:, at] = (cot_ref[:, at].astype(F32) * gelu_slope(preact)).astype(BF16)
    first = jnp.zeros((rows, 1), F32)
    second = jnp.zeros((rows, 1), F32)
    for is_mine in (False, True):
        at_half = half if is_mine else 1 - half
        for start in range(0, columns, tile):
            features = pl.ds(pl.multiple_of(at_half * columns + start, tile), tile)
            part = lax.dot_general(
                grad_ref[...], weight_ref[features, :], (((1,), (1,)), ((), ())), preferred_element_type=F32
            )
            first += jnp.sum(part, axis=-1, keepdims=True)
            second += jnp.sum(part * normed_ref[:, features].astype(F32), axis=-1, keepdims=True)
            if is_mine:
                keep_ref[:, start : start + tile] = part
            else:
                send_ref[:, start : start + tile] = part.astype(BF16)
    lane = lax.broadcasted_iota(jnp.int32, (rows, 128), 1)
    left = jnp.where(lane < 64, first, second)
    sums_ref[...] = left
    terms = jnp.zeros((rows, 128), F32)
    for index in range(3):
        term = left.astype(BF16).astype(F32)
        left = left - term
        terms = jnp.where(lane % 64 // 16 == index, term, terms)
    send_ref[:, columns : columns + 128] = terms.astype(BF16)


def backward_rows(place, normed, weight, cot, tokens=()):
    rows, columns = cot.shape
    outs = [array(rows, columns), array(rows, columns + 128), array(rows, columns, F32), array(rows, 128, F32)]
    return call(backward_kernel, "backward_rows", place, [normed, weight, cot], outs, tokens)


def stack_kernel(place_ref, *refs):
    rows = refs[0].shape[0]
    for index, ref in enumerate(refs[:-1]):
        refs[-1][index * rows : (index + 1) * rows, :] = ref[...]


def stack(place, values, tokens=()):
    rows, columns = values[0].shape
    return call(stack_kernel, "stack_blocks", place, values, [array(len(values) * rows, columns)], tokens)[0]


def load_kernel(place_ref, weight_ref, held_ref, sem):
    copy = pltpu.make_async_copy(weight_ref, held_ref, sem)
    copy.start()
    copy.wait()


def load(place, weight):
    held = pl.pallas_call(
        load_kernel,
        in_specs=[SMEM, ANY],
        out_specs=VMEM,
        out_shape=pltpu.VMEM(weight.shape, weight.dtype),
        scratch_shapes=[pltpu.SemaphoreType.DMA],
        compiler_params=pltpu.CompilerParams(vmem_limit_bytes=VMEM_LIMIT),
        name="load_weights",
    )(place, weight)
    return pltpu.with_memory_space_constraint(held, pltpu.VMEM)


def forward_kernel(place_ref, own_ref, other_ref, weight_ref, out_ref, normed_ref, tile=256):
    normalize_into(own_ref, other_ref, normed_ref, place_ref[1])
    for start in range(0, out_ref.shape[1], tile):
        at = slice(start, start + tile)
        preact = jnp.dot(normed_ref[...], weight_ref[:, at], preferred_element_type=F32)
        out_ref[:, at] = (own_ref[:, at].astype(F32) + gelu(preact)).astype(BF16)


def forward_layer(place, own, other, weight, tokens=()):
    scratch = [pltpu.VMEM((own.shape[0], weight.shape[0]), BF16)]
    return call(
        forward_kernel, "forward_layer", place, [own, other, weight], [array(*own.shape)], tokens, scratch
    )[0]


def input_grad_kernel(
    place_ref, cot_ref, keep_ref, arrived_ref, sums_ref, inverse_ref, scaled_ref, out_ref
):
    columns = cot_ref.shape[1]
    depth = 2 * columns
    terms = arrived_ref[:, columns : columns + 128].astype(F32)
    first = sums_ref[:, 0:1] + ((terms[:, 0:1] + terms[:, 16:17]) + terms[:, 32:33])
    second = sums_ref[:, 64:65] + ((terms[:, 64:65] + terms[:, 80:81]) + terms[:, 96:97])
    dnormed = keep_ref[...] + arrived_ref[:, :columns].astype(F32)
    scaled = scaled_ref[...].astype(F32)
    out_ref[...] = (
        cot_ref[...].astype(F32)
        + inverse_ref[:, 0:1] * (dnormed - first / depth - scaled * (second / depth))
    ).astype(BF16)


def input_grads(place, cot, keep, arrived, sums, inverse, scaled, tokens=()):
    values = [cot, keep, arrived, sums, inverse, scaled]
    return call(input_grad_kernel, "input_grads", place, values, [array(*cot.shape)], tokens)[0]


def gather_kernel(replicas, place_ref, own_ref, *refs):
    near_refs, (far_ref, out_ref, blocks) = refs[: replicas - 1], refs[replicas - 1 :]
    rows = own_ref.shape[0]
    part = rows // 2
    half = place_ref[1]
    blocks[:rows, :] = own_ref[...]
    for steps in range(1, replicas):
        near = pl.ds(pl.multiple_of(rows * steps + half * part, part), part)
        far = pl.ds(pl.multiple_of(rows * steps + (1 - half) * part, part), part)
        blocks[near, :] = near_refs[steps - 1][...]
        blocks[far, :] = far_ref[(steps - 1) * part : steps * part, :]
    out_ref[...] = blocks[...].T


def gather_blocks(place, own, near, far):
    replicas = len(near) + 1
    rows, block = own.shape
    kernel = functools.partial(gather_kernel, replicas)
    scratch = [pltpu.VMEM((replicas * rows, block), BF16)]
    outs = [array(block, replicas * rows)]
    return call(
        kernel, "gather_blocks", place, [own, *near, far], outs, (), scratch
    )[0]


def gather_grad_kernel(place_ref, own_ref, *refs):
    *refs, out_ref = refs
    others = len(refs) // 2
    rows = own_ref.shape[0]
    out_ref[:rows, :] = own_ref[...]
    for steps in range(1, others + 1):
        out_ref[rows * steps : rows * (steps + 1), :] = jnp.where(
            place_ref[0] >= steps, refs[steps - 1][...], refs[others + steps - 1][...]
        )


def gather_grads(place, own, ups, downs):
    values = [own, *ups, *downs]
    outs = [array((len(ups) + 1) * own.shape[0], own.shape[1])]
    return call(
        gather_grad_kernel, "gather_grads", place, values, outs, limit=16 * 2**20, flops=3 * 10**10
    )[0]


def weight_grad_kernel(passed, place_ref, *refs, width=512):
    blocks_ref, grads_ref, *refs = refs
    pass_refs, out_ref, pass_outs = refs[:passed], refs[passed], refs[passed + 1 : 2 * passed + 1]
    held, sems, pass_sems = refs[-3:]
    passing = [
        pltpu.make_async_copy(pass_refs[at], pass_outs[at], pass_sems.at[at]) for at in range(passed)
    ]
    for copy in passing:
        copy.start()
    stores = []
    for index, start in enumerate(range(0, grads_ref.shape[1], width)):
        at = slice(start, start + width)
        held[:, at] = jnp.dot(
            blocks_ref[...], grads_ref[:, at], preferred_element_type=F32
        ).astype(BF16)
        stores.append(pltpu.make_async_copy(held.at[:, at], out_ref.at[:, at], sems.at[index]))
        stores[-1].start()
    for copy in stores + passing:
        copy.wait()


def weight_grads(place, blocks, grads, passes, width=512, limit=20 * 2**20):
    block, columns = blocks.shape[0], grads.shape[1]
    outs = [array(block, columns)] + [array(*value.shape) for value in passes]
    return pl.pallas_call(
        functools.partial(weight_grad_kernel, len(passes), width=width),
        in_specs=[SMEM] + [VMEM] * (2 + len(passes)),
        out_specs=[ANY] * len(outs),
        out_shape=outs,
        scratch_shapes=[
            pltpu.VMEM((block, columns), BF16),
            pltpu.SemaphoreType.DMA((columns // width,)),
            pltpu.SemaphoreType.DMA((len(passes),)),
        ],
        compiler_params=pltpu.CompilerParams(vmem_limit_bytes=limit),
        cost_estimate=pl.CostEstimate(flops=1000, bytes_accessed=1000, transcendentals=0),
        name="weight_grads",
    )(place, blocks, grads, *passes)


def after(value, *others):
    return lax.optimization_barrier((value, *others))[0]


def body(act_in, weights, act_saved, cotangent):
    weight = weights[0]
    own_in, own_saved, own_cot = act_in[0], act_saved[0], cotangent[0]
    replicas = lax.axis_size("dp")
    place = jnp.stack([lax.axis_index("dp"), lax.axis_index("mp")]).astype(jnp.int32)

    other_saved = swap(own_saved, "mp")
    weight = load(place, weight)
    other_in = swap(after(own_in, weight), "mp")

    normed, inverse, scaled, own_block, *blocks = norm_rows(
        place, own_saved, other_saved, replicas, [weight]
    )
    near = [shift(block, "dp", steps + 1) for steps, block in enumerate(blocks)]
    grad, send, keep, sums = backward_rows(place, normed, weight, own_cot)

    grad = after(grad, *near)
    arrived = swap(after(send, other_in, *near), "mp")
    ups, downs = [grad], [grad]
    for steps in range(1, replicas):
        if steps <= replicas // 2:
            ups.append(along(ups[-1], "dp", 1, steps - 1))
            downs.append(along(downs[-1], "dp", -1, steps - 1))
        else:
            ups.append(across(grad, "dp", steps))
            downs.append(ups[-1])

    forward = forward_layer(place, own_in, other_in, weight)
    received = shift(after(forward, *near), "section", 1)
    received_other = shift_and_swap(after(forward, arrived), 1)

    far = swap(after(stack(place, near), received_other), "mp")
    shadow_there = forward_layer(place, received, received_other, weight)
    shadow = shift(shadow_there, "section", -1)

    input_grad = input_grads(place, own_cot, keep, arrived, sums, inverse, scaled)
    grad_back = shift(after(input_grad, received_other), "section", -1)

    weight_grad, received, shadow, grad_back = weight_grads(
        place,
        gather_blocks(place, own_block, near, far),
        gather_grads(place, grad, ups[1:], downs[:0:-1]),
        [received, shadow, grad_back],
    )
    return (received[None], shadow[None], grad_back[None], weight_grad[None])


def solution(mesh):
    return jax.shard_map(
        body,
        mesh=mesh,
        in_specs=(
            P("section", "dp", "mp"),
            P("section", None, "mp"),
            P("section", "dp", "mp"),
            P("section", "dp", "mp"),
        ),
        out_specs=(
            P("section", "dp", "mp"),
            P("section", "dp", "mp"),
            P("section", "dp", "mp"),
            P("section", "dp", "mp"),
        ),
        check_vma=False,
    )
```
